128 devices in a mesh: rows: 32 (over z_lo, x, y), cols: 4 (over z_hi, core).
Axes of the slice: x: 4, y: 4, z: 4 (z_hi: 2, z_lo: 2; z = z_hi * 2 + z_lo), core: 2. Of those that a mesh axis runs over, the one named last changes fastest.
Arguments:
- anchors: bfloat16 [32768, 8192], P('rows', 'cols'), may hold values from -64 to 64
- targets: bfloat16 [32768, 512], P('rows', 'cols'), may hold values from -6 to 6
- holdout: bfloat16 [8192, 8192], P('rows', 'cols'), may hold values from -64 to 64
Outputs:
- predicted: float32 [8192, 512], P('rows', 'cols')
The draws below stay inside these ranges and needn't reach their ends.
All inputs are finite; a program needn't handle non-finite values.
Results may differ from the reference program's by a relative error of at most 0.01.
Values may be sent and summed in bfloat16 or wider, within the bound.
No kernel may reach another device: no remote copies, remote signals or barrier semaphores. Data moves between devices by JAX's collectives and lax.ppermute only.
A program may use at most 128 MiB of HBM per device.

```python
import math
import jax
import jax.numpy as jnp
from jax import lax

D = 8192
K = 512
ANCHORS = 32768
HOLDOUT = 8192


value_bound = 64.0


def feature_scale(key):
    top_log = math.log(1.5)
    return jnp.exp(jax.random.uniform(jax.random.fold_in(key, 101), (D,), jnp.float32, 0.0, top_log))


def scaled_rows(key, amount, salt):
    own_key = jax.random.fold_in(key, salt)
    rising = jnp.exp(math.log(2.0) * jnp.arange(amount, dtype=jnp.float32) / amount)
    jitter = jnp.exp(jax.random.uniform(jax.random.fold_in(own_key, 1), (amount,), jnp.float32, 0.0, math.log(2.0)))
    values = jnp.clip(jax.random.normal(jax.random.fold_in(own_key, 2), (amount, D), jnp.float32), -6.0, 6.0)
    scaled = 0.5 * values * (rising * jitter)[:, None] * feature_scale(key)[None, :]
    return jnp.clip(scaled, -value_bound, value_bound).astype(jnp.bfloat16)


def draw_anchors(key, part):
    return scaled_rows(key, ANCHORS, 202)


def draw_holdout(key, part):
    return scaled_rows(key, HOLDOUT, 303)


def shard_levels(stream_key, extent, shards, low, top_value):
    level, own = 1.0, jax.random.fold_in(stream_key, 6)
    for position, parts in shards:
        heights = jnp.exp(jax.random.uniform(jax.random.fold_in(own, position), (parts,), jnp.float32, low / len(shards), top_value / len(shards)))
        level = level * jnp.repeat(heights, extent[position] // parts).reshape([-1 if axis == position else 1 for axis in range(len(extent))])
    return level


def noise(key, dims, width, most, split=(), held_as=jnp.bfloat16):
    factor_of = shard_levels(key, dims, split, -0.22, 0.18) if split else 1.0
    values = jax.random.normal(key, dims, jnp.float32) * width * factor_of
    return jnp.minimum(jnp.maximum(values, -most), most).astype(held_as)


def setup_inputs(seed: int = 0) -> dict:
    splits = jax.random.split(jax.random.key(seed), 4)
    anchors = draw_anchors(jax.random.fold_in(splits[3], 71), 0)
    targets = noise(splits[1], (ANCHORS, K), 1.0, 6.0, ((0, 32), (1, 4)))
    holdout = draw_holdout(jax.random.fold_in(splits[3], 71), 0)
    return {"anchors": anchors, "targets": targets, "holdout": holdout}


ridge_weight = 1.0

def gram_of(left_mat, right_mat):
    return lax.dot_general(left_mat.astype(jnp.float32), right_mat.astype(jnp.float32), (((0,), (0,)), ((), ())), precision=lax.Precision.HIGHEST, preferred_element_type=jnp.float32)

def combine_cols(block_mat, small_mat):
    return jnp.dot(block_mat.astype(jnp.float32), small_mat.astype(jnp.float32), precision=lax.Precision.HIGHEST, preferred_element_type=jnp.float32)

def symmetric(matrix):
    return 0.5 * (matrix + matrix.T)

def solve_spd(matrix, right_side):
    factor = jnp.linalg.cholesky(matrix)
    return jax.scipy.linalg.cho_solve((factor, True), right_side)

def normal_apply(anchors, direction):
    low_copy = direction.astype(jnp.bfloat16)
    images = jnp.dot(anchors.astype(jnp.float32), low_copy.astype(jnp.float32), preferred_element_type=jnp.float32).astype(jnp.bfloat16)
    normal_back = lax.dot_general(anchors.astype(jnp.float32), images.astype(jnp.float32), (((0,), (0,)), ((), ())), preferred_element_type=jnp.float32)
    return normal_back / ANCHORS + ridge_weight * direction

def reference(anchors, targets, holdout):
    start_sum = lax.dot_general(anchors.astype(jnp.float32), targets.astype(jnp.float32), (((0,), (0,)), ((), ())), preferred_element_type=jnp.float32)
    residual = start_sum / ANCHORS
    direction = residual
    res_gram = gram_of(residual, residual)
    image_dir = normal_apply(anchors, direction)
    step_alpha = solve_spd(symmetric(gram_of(direction, image_dir)), res_gram)
    fitted = combine_cols(direction, step_alpha)
    residual = residual - combine_cols(image_dir, step_alpha)
    next_gram = gram_of(residual, residual)
    step_beta = solve_spd(symmetric(res_gram), next_gram)
    direction = residual + combine_cols(direction, step_beta)
    image_dir = normal_apply(anchors, direction)
    step_alpha = solve_spd(symmetric(gram_of(direction, image_dir)), next_gram)
    fitted = fitted + combine_cols(direction, step_alpha)
    fitted_low = fitted.astype(jnp.bfloat16)
    return jnp.dot(holdout.astype(jnp.float32), fitted_low.astype(jnp.float32), preferred_element_type=jnp.float32)
```

```python
import functools

import jax
import jax.numpy as jnp
from jax import lax
from jax.experimental import pallas as pl
from jax.experimental.pallas import tpu as pltpu
from jax.sharding import PartitionSpec as P

ridge_weight = 1.0
low = jnp.bfloat16
full = jnp.float32
exact = lax.Precision.HIGHEST


def sibling(value):
    return lax.ppermute(value, "cols", [(c, c ^ 1) for c in range(4)])


def across(value):
    return lax.ppermute(value, "cols", [(c, c ^ 2) for c in range(4)])


def moved(value, step):
    pairs = []
    for r in range(32):
        z, x, y = r // 16, r // 4 % 4, r % 4
        to = ((z + step[0]) % 2 * 4 + (x + step[1]) % 4) * 4 + (y + step[2]) % 4
        pairs.append((r, to))
    return lax.ppermute(value, "rows", pairs)


def in_order(first, mine, other, axis):
    return jnp.where(
        first, jnp.concatenate([mine, other], axis), jnp.concatenate([other, mine], axis)
    )


def along_x(step):
    return (0, step, 0)


def sum_over_x(value, place):
    tiles = [
        lax.dynamic_index_in_dim(value, (place + step) % 4, 0, keepdims=False).astype(low)
        for step in range(4)
    ]
    arrived = [moved(tiles[step], along_x(step)) for step in (2, 1, 3)]
    return sum([piece.astype(full) for piece in arrived], tiles[0].astype(full))


def sum_over_y_z(value, y_type):
    sent = value.astype(y_type)
    arrived = [moved(sent, (0, 0, step)) for step in (2, 1, 3)]
    value = sum([piece.astype(full) for piece in arrived], sent.astype(full))
    return value + moved(value, (1, 0, 0))


def gather_over_x(value, place):
    arrived = {step: moved(value, along_x(step)) for step in (2, 1, 3)}
    tiles = jnp.zeros((4, *value.shape), value.dtype)
    for step, tile in ((0, value), *arrived.items()):
        tiles = lax.dynamic_update_index_in_dim(tiles, tile, (place + 4 - step) % 4, 0)
    return tiles


def after(value, *others):
    return lax.optimization_barrier((value, *others))[0]


def dot_t(left, right):
    return lax.dot_general(
        left, right, (((0,), (0,)), ((), ())), preferred_element_type=full
    )


def dot(left, right):
    return jnp.dot(left, right, preferred_element_type=full)


def dot_exact(left, right):
    return jnp.dot(left, right, precision=exact, preferred_element_type=full)


def split(value):
    high = value.astype(low)
    return high, (value - high.astype(full)).astype(low)


def dot3(left, right):
    left_high, left_low = split(left)
    right_high, right_low = split(right)
    return dot(left_high, right_high) + (dot(left_high, right_low) + dot(left_low, right_high))


def inverse_kernel(m_ref, x_ref, b_ref):
    size = m_ref.shape[0]
    at_row = lax.broadcasted_iota(jnp.int32, (size, size), 0)
    at_col = lax.broadcasted_iota(jnp.int32, (size, size), 1)
    eye = (at_row == at_col).astype(full)
    diagonal = m_ref[...] * eye
    scale_col = lax.rsqrt(jnp.sum(diagonal, axis=1, keepdims=True))
    scale_row = lax.rsqrt(jnp.sum(diagonal, axis=0, keepdims=True))
    b_ref[...] = m_ref[...] * scale_col * scale_row
    b_low = b_ref[...].astype(low)
    square = dot(b_low, b_low)
    square_low = square.astype(low)
    fourth = dot(square_low, square_low)
    bound = jnp.sqrt(jnp.sqrt(jnp.sqrt(jnp.sum(fourth * fourth))))
    c = 1.85 / bound
    x_ref[...] = 2.0 * c * eye - (c * c) * b_ref[...]

    def not_yet(state):
        step, left_over = state
        return jnp.logical_and(step < 48, left_over > 1e-7)

    def improve(state):
        step, _ = state
        x = x_ref[...]
        residual = eye - dot3(b_ref[...], x)
        x_ref[...] = x + dot(x.astype(low), residual.astype(low))
        return step + 1, jnp.sum(residual * residual)

    lax.while_loop(not_yet, improve, (jnp.int32(0), jnp.float32(1.0)))
    x_ref[...] = x_ref[...] * scale_col * scale_row


def inverse(matrix):
    size = matrix.shape[0]
    return pl.pallas_call(
        inverse_kernel,
        out_shape=jax.ShapeDtypeStruct((size, size), full),
        in_specs=[pl.BlockSpec(memory_space=pltpu.VMEM)],
        out_specs=pl.BlockSpec(memory_space=pltpu.VMEM),
        scratch_shapes=[pltpu.VMEM((size, size), full)],
        compiler_params=pltpu.CompilerParams(vmem_limit_bytes=12 * 1024 * 1024),
        cost_estimate=pl.CostEstimate(
            flops=2 * size**3, bytes_accessed=8 * size**2, transcendentals=0
        ),
    )(matrix)


def symmetric(matrix):
    return 0.5 * (matrix + matrix.T)


def on_device(anchors, targets, holdout):
    rows_dev = anchors.shape[0]
    n_rows = lax.axis_size("rows")
    anchors_all = rows_dev * n_rows
    col = lax.axis_index("cols")
    high, core = col // 2, col % 2
    at_x = lax.axis_index("rows") // 4 % 4
    z_first, c_first = high == 0, core == 0
    width = targets.shape[1]
    start = (core * 2 + high) * width

    both_anchors = jnp.concatenate([anchors, sibling(anchors)], axis=1)
    both_holdout = jnp.concatenate([holdout, sibling(holdout)], axis=1)
    mine = in_order(z_first, targets, across(targets), 1)
    targets_full = in_order(c_first, mine, sibling(mine), 1)
    mine, both_holdout, targets_full = lax.optimization_barrier(
        (mine, both_holdout, targets_full)
    )
    n_feat = both_anchors.shape[1]

    def tiles_of(images):
        partial_sum = dot_t(both_anchors, images)
        return partial_sum.astype(low).reshape(n_rows, n_feat // n_rows, -1)

    def exchanged(tiles):
        return lax.all_to_all(tiles, "rows", 0, 0, tiled=True)

    def summed(arrived):
        return arrived.astype(full).sum(axis=0) / anchors_all

    def copies_of(share):
        return jnp.broadcast_to(share.astype(low), (n_rows, *share.shape))

    def applied(block):
        return dot(both_anchors, block)

    def with_across(part):
        return part + across(part.astype(low)).astype(full)

    def all_columns(block):
        return in_order(c_first, block, sibling(block), 1)

    def with_pair(tile):
        return in_order(z_first, tile[None], across(tile)[None], 0)

    def whole(pair):
        size = pair.shape[2]
        rows = gather_over_x(pair, at_x)
        rows = rows.reshape(2, 2, 2, -1, size).transpose(0, 2, 1, 3, 4).reshape(2, 2 * width, size)
        rows = in_order(c_first, rows, sibling(rows), 1)
        return rows[0] / anchors_all, rows[1] / anchors_all

    residual_share = summed(exchanged(tiles_of(mine)))
    direction = exchanged(copies_of(residual_share)).reshape(n_feat, -1)
    images = with_across(applied(direction)).astype(low)

    tiles = tiles_of(images)
    arrived = exchanged(tiles)
    images_own = lax.dynamic_slice_in_dim(images, high * width, width, 1)
    images_full = all_columns(images)
    gram = jnp.stack([dot_t(images_own, targets_full), dot_t(images_own, images_full)])
    gram = after(gram, tiles)
    gram = with_pair(sum_over_y_z(sum_over_x(gram.reshape(4, width // 2, -1), at_x), full))

    copies = copies_of(summed(arrived) + ridge_weight * residual_share)
    gram, copies = lax.optimization_barrier((gram, copies))
    image_dir = exchanged(copies).reshape(n_feat, -1)
    gram_t, gram_y = whole(gram)
    held_dir = dot(both_holdout, after(direction, copies))
    held_dir = all_columns(held_dir + across(held_dir))
    gram_y, held_dir = lax.optimization_barrier((gram_y, held_dir))
    res_gram = symmetric(gram_t)
    energy = symmetric(gram_y) + res_gram
    energy_inv = inverse(energy)
    alpha0 = dot_exact(energy_inv, res_gram)
    alpha_high, alpha_low = split(alpha0)

    second = all_columns(with_across(applied(image_dir)).astype(low))
    res_images = images_full.astype(full) - (dot(second, alpha_high) + dot(second, alpha_low))
    res_images = res_images.astype(low)
    res_own = lax.dynamic_slice_in_dim(res_images, start, width, 1)
    gram = jnp.stack([dot_t(res_own, res_images), dot_t(images_own, res_images)])
    gram = sum_over_x(gram.reshape(4, width // 2, -1), at_x)

    held_image = dot(both_holdout, image_dir)
    held_image = held_image + across(after(held_image, second))
    held_image = all_columns(held_image)
    gram, held_image = lax.optimization_barrier((gram, held_image))
    gram_w, gram_b = whole(with_pair(sum_over_y_z(gram, low)))

    held_res = held_dir - dot_exact(held_image, alpha0)
    beta0 = -dot_exact(energy_inv, gram_b)
    next_gram = -symmetric(dot_exact(gram_b.T, alpha0))
    next_energy = symmetric(gram_w + next_gram + dot_exact(gram_b.T, beta0))
    next_own = lax.dynamic_slice_in_dim(next_gram, start, width, 1)
    alpha1_own = dot_exact(inverse(next_energy), next_own)
    alpha0_own = lax.dynamic_slice_in_dim(alpha0, start, width, 1)
    held_next = held_res + dot_exact(held_dir, beta0)
    return dot_exact(held_dir, alpha0_own) + dot_exact(held_next, alpha1_own)


def solution(mesh):
    placed = (P("rows", "cols"), P("rows", "cols"), P("rows", "cols"))
    return jax.shard_map(
        on_device, mesh=mesh, in_specs=placed, out_specs=P("rows", "cols"), check_vma=False
    )
```
